32 devices in a mesh: row: 4 (over y, x), col: 8 (over z, core).
Axes of the slice: x: 2, y: 2, z: 4, core: 2. Of those that a mesh axis runs over, the one named last changes fastest.
Arguments:
- voltages: bfloat16 [2, 64, 64, 2, 31744], P(None, 'row', 'col'), may hold values from -6 to 6
- fir: float32 [16, 1024], replicated, may hold values from -0.046875 to 0.046875
Outputs:
- power: float32 [64, 64, 2, 1024], P('col', None, None, 'row')
The draws below stay inside these ranges and needn't reach their ends.
All inputs are finite; a program needn't handle non-finite values.
Results may differ from the reference program's by a relative error of at most 0.0032.
Values may be sent and summed in bfloat16 or wider, within the bound.
A program may use at most 448 MiB of HBM per device.

```python
import math
import jax
import jax.numpy as jnp
from jax import lax

NROW = 64
NCOL = 64
POL = 2
NCHAN = 1024
TAPS = 16
FRAMES = 16
SAMPLES = 31744


def shard_levels(rng, extent, cuts, smallest, high):
    gain = 1.0
    for dim, parts in cuts:
        steps = jax.random.uniform(jax.random.fold_in(jax.random.fold_in(rng, 6), dim), (parts,), jnp.float32, smallest / len(cuts), high / len(cuts))
        gain = gain * jnp.repeat(jnp.exp(steps), extent[dim] // parts).reshape((-1,) + (1,) * (len(extent) - 1 - dim))
    return gain


def bell_draw(key, dims, scale, limit, split=(), kind=jnp.bfloat16):
    values = jax.random.normal(key, dims, jnp.float32) * scale
    if len(split) > 0:
        values = shard_levels(key, dims, split, -0.22, 0.18) * values
    return jnp.clip(values, min=-limit, max=limit).astype(kind)


def setup_inputs(seed: int = 0) -> dict:
    keys = jax.random.split(jax.random.key(seed), 3)
    return {
        "voltages": bell_draw(keys[0], (2, NROW, NCOL, POL, SAMPLES), 1.0, 6.0, ((1, 4), (2, 8))),
        "fir": bell_draw(keys[1], (TAPS, NCHAN), (TAPS * NCHAN) ** -0.5, 0.046875, (), jnp.float32),
    }


def spatial_table(length):
    index = jnp.arange(length, dtype=jnp.int32)
    angle = ((index[:, None] * index[None, :]) % length).astype(jnp.float32) * (2.0 * math.pi / length)
    cosine = jnp.cos(angle).astype(jnp.bfloat16)
    sine = jnp.sin(angle).astype(jnp.bfloat16)
    return jnp.stack([jnp.stack([cosine, -sine]), jnp.stack([sine, cosine])])


def channelize_row(volt_row, fir):
    shaped = volt_row.reshape(2, NCOL, POL, FRAMES + TAPS - 1, NCHAN)
    filtered = jnp.zeros((2, NCOL, POL, FRAMES, NCHAN), jnp.float32)
    for tap in range(TAPS):
        filtered = filtered + shaped[:, :, :, tap:tap + FRAMES, :].astype(jnp.float32) * fir[tap]
    spectrum = jnp.fft.fft(lax.complex(filtered[0], filtered[1]), axis=-1)
    return jnp.stack([jnp.real(spectrum), jnp.imag(spectrum)]).astype(jnp.bfloat16)


def reference(voltages, fir):
    by_row = jnp.moveaxis(voltages, 1, 0)
    spectra = lax.map(lambda volt_row: channelize_row(volt_row, fir), by_row)
    per_frame = jnp.moveaxis(spectra, 4, 0)
    row_tab = spatial_table(NROW).astype(jnp.float32)
    col_tab = spatial_table(NCOL).astype(jnp.float32)

    def frame_step(total, frame_data):
        rowbeam = jnp.einsum("xcbpk,cdux->dubpk", frame_data.astype(jnp.float32), row_tab).astype(jnp.bfloat16)
        beams = jnp.einsum("cubpk,cdvb->duvpk", rowbeam.astype(jnp.float32), col_tab)
        return total + jnp.sum(beams * beams, axis=0), None

    start = jnp.zeros((NROW, NCOL, POL, NCHAN), jnp.float32)
    total, _ = lax.scan(frame_step, start, per_frame)
    return total * (1.0 / (FRAMES * NROW * NCOL))
```

```python
import functools
import math

import jax
import jax.numpy as jnp
import numpy as np
import ml_dtypes
from jax import lax
from jax.experimental import pallas as pl
from jax.experimental.pallas import tpu as pltpu
from jax.sharding import PartitionSpec as P

BF16 = jnp.bfloat16
F32 = jnp.float32
MESH = pl.DeviceIdType.MESH
VMEM_BYTES = 58 * 1024 * 1024
SLOTS = 3
CHUNKS = 8


def fourier_parts(length):
    index = np.arange(length)
    angle = (index[:, None] * index[None, :] % length).astype(np.float32) * np.float32(
        2.0 * math.pi / length
    )
    return np.cos(angle), np.sin(angle)


def channel_table(nchan, row_size):
    cosine, sine = fourier_parts(nchan)
    table = np.stack([np.stack([cosine, -sine]), np.stack([sine, cosine])])
    table = table.reshape(2, 2, nchan, row_size, nchan // row_size).transpose(0, 2, 3, 1, 4)
    return table.reshape(2 * nchan, 2 * nchan).astype(ml_dtypes.bfloat16)


def spatial_parts(length):
    cosine, sine = fourier_parts(length)
    table = np.stack([np.stack([cosine, -sine]), np.stack([sine, cosine])])
    return table.astype(ml_dtypes.bfloat16)


def row_table(nrow, row_size, col_size):
    table = spatial_parts(nrow).reshape(2, 2, col_size, nrow // col_size, row_size, nrow // row_size)
    return table.transpose(2, 1, 3, 4, 0, 5).reshape(2 * nrow, 2 * nrow)


def col_table(ncol, col_size, local_beams):
    table = spatial_parts(ncol).astype(np.float32)
    eye = np.eye(local_beams, dtype=np.float32)
    full = np.einsum("cdvb,uw->duvbcw", table, eye)
    return full.reshape(2 * local_beams * ncol, ncol * 2 * local_beams).astype(ml_dtypes.bfloat16)


def channelize_kernel(volts, fir, table, out, held):
    _, _, _, blocks, rows, nchan = volts.shape
    taps = fir.shape[0]
    frames = blocks - taps + 1
    lanes = 128
    steps = nchan // lanes

    def filter_step(step, carry):
        comp = step // steps
        start = pl.multiple_of((step % steps) * lanes, lanes)
        weights = [
            jnp.broadcast_to(fir[pl.ds(tap, 1), pl.ds(start, lanes)], (rows, lanes))
            for tap in range(taps)
        ]
        values = [
            volts[0, 0, comp, block, :, pl.ds(start, lanes)].astype(F32) for block in range(blocks)
        ]
        dest = pl.multiple_of(step * lanes, lanes)
        for frame in range(frames):
            total = values[frame] * weights[0]
            for tap in range(1, taps):
                total = total + values[frame + tap] * weights[tap]
            held[frame, :, pl.ds(dest, lanes)] = total.astype(BF16)
        return carry

    lax.fori_loop(0, 2 * steps, filter_step, 0)
    width = out.shape[-1]
    filtered = held[...].reshape(frames * rows, 2 * nchan)

    for dest in range(out.shape[0]):
        for comp in range(2):
            start = (2 * dest + comp) * width
            part = jnp.dot(
                filtered, table[:, start : start + width], preferred_element_type=F32
            ).astype(BF16)
            out[dest, 0, :, 0, comp * rows : (comp + 1) * rows, :] = part.reshape(frames, rows, width)


def channelize(volts, fir, table, row_size):
    pols, local_cols, _, blocks, local_rows, nchan = volts.shape
    taps = fir.shape[0]
    frames = blocks - taps + 1
    width = nchan // row_size
    return pl.pallas_call(
        channelize_kernel,
        grid=(pols, local_cols),
        in_specs=[
            pl.BlockSpec((1, 1, 2, blocks, local_rows, nchan), lambda p, b: (p, b, 0, 0, 0, 0)),
            pl.BlockSpec((taps, nchan), lambda p, b: (0, 0)),
            pl.BlockSpec((2 * nchan, 2 * nchan), lambda p, b: (0, 0)),
        ],
        out_specs=pl.BlockSpec(
            (row_size, 1, frames, 1, 2 * local_rows, width), lambda p, b: (0, p, 0, b, 0, 0)
        ),
        out_shape=jax.ShapeDtypeStruct(
            (row_size, pols, frames, local_cols, 2 * local_rows, width), BF16
        ),
        scratch_shapes=[pltpu.VMEM((frames, local_rows, 2 * nchan), BF16)],
        compiler_params=pltpu.CompilerParams(vmem_limit_bytes=VMEM_BYTES),
        name="channelize",
    )(volts, fir, table)


def beam_kernel(
    row_size, col_size, chunks, spectra, row_tab, col_tab, power,
    row_recv, col_send, col_recv,
    row_send_sem, row_recv_sem, row_own_sem, col_send_sem, col_recv_sem, col_own_sem,
):
    my_row = lax.axis_index("row")
    my_col = lax.axis_index("col")
    units = spectra.shape[1]
    local_cols = spectra.shape[2]
    width = spectra.shape[4]
    size = units // chunks
    per_pol = units // power.shape[0]
    out_rows = power.shape[1]
    row_peers = [lax.rem(my_row + step, row_size) for step in range(1, row_size)]
    col_peers = [lax.rem(my_col + step, col_size) for step in range(1, col_size)]

    def row_copy(chunk, peer, source):
        part = pl.ds(chunk * size, size)
        return pltpu.make_async_remote_copy(
            src_ref=spectra.at[peer, part],
            dst_ref=row_recv.at[source, part],
            send_sem=row_send_sem.at[chunk, peer],
            recv_sem=row_recv_sem.at[chunk, source],
            device_id={"row": peer},
            device_id_type=MESH,
        )

    def row_own(chunk):
        part = pl.ds(chunk * size, size)
        return pltpu.make_async_copy(
            spectra.at[my_row, part], row_recv.at[my_row, part], row_own_sem.at[chunk]
        )

    def col_copy(chunk, peer, source):
        slot = lax.rem(chunk, SLOTS)
        return pltpu.make_async_remote_copy(
            src_ref=col_send.at[slot, peer],
            dst_ref=col_recv.at[source, pl.ds(chunk * size, size)],
            send_sem=col_send_sem.at[chunk, peer],
            recv_sem=col_recv_sem.at[chunk, source],
            device_id={"col": peer},
            device_id_type=MESH,
        )

    def col_own(chunk):
        return pltpu.make_async_copy(
            col_send.at[lax.rem(chunk, SLOTS), my_col],
            col_recv.at[my_col, pl.ds(chunk * size, size)],
            col_own_sem.at[chunk],
        )

    def start_row(chunk):
        for peer in row_peers:
            row_copy(chunk, peer, my_row).start()
        row_own(chunk).start()

    def combine(chunk):
        for peer in col_peers:
            col_copy(chunk, peer, peer).wait_recv()
        col_own(chunk).wait()

        def unit_step(step, carry):
            unit = chunk * size + step
            pol = unit // per_pol
            block = col_recv[:, unit].reshape(-1, width)
            real = jnp.dot(col_tab[:out_rows], block, preferred_element_type=F32)
            imag = jnp.dot(col_tab[out_rows:], block, preferred_element_type=F32)
            power[pol] += real * real + imag * imag
            return carry

        lax.fori_loop(0, size, unit_step, 0)

    barrier = pltpu.get_barrier_semaphore()
    for peer in row_peers:
        pl.semaphore_signal(barrier, inc=1, device_id={"row": peer}, device_id_type=MESH)
    for peer in col_peers:
        pl.semaphore_signal(barrier, inc=1, device_id={"col": peer}, device_id_type=MESH)
    pl.semaphore_wait(barrier, row_size + col_size - 2)

    power[...] = jnp.zeros_like(power)
    start_row(0)
    start_row(1)

    def chunk_step(chunk, carry):
        for peer in row_peers:
            row_copy(chunk, peer, peer).wait_recv()
        row_own(chunk).wait()

        @pl.when(chunk + 2 < chunks)
        def _():
            start_row(chunk + 2)

        @pl.when(chunk >= SLOTS)
        def _():
            for peer in col_peers:
                col_copy(chunk - SLOTS, peer, my_col).wait_send()

        slot = lax.rem(chunk, SLOTS)

        def unit_step(step, inner):
            for column in range(local_cols):
                block = row_recv[:, chunk * size + step, column].reshape(-1, width)
                beam = jnp.dot(row_tab[...], block, preferred_element_type=F32).astype(BF16)
                col_send[slot, :, step, column] = beam.reshape(col_size, -1, width)
            return inner

        lax.fori_loop(0, size, unit_step, 0)
        for peer in col_peers:
            col_copy(chunk, peer, my_col).start()
        col_own(chunk).start()

        @pl.when(chunk >= 1)
        def _():
            combine(chunk - 1)

        return carry

    lax.fori_loop(0, chunks, chunk_step, 0)
    combine(chunks - 1)

    def drain_row(chunk, carry):
        for peer in row_peers:
            row_copy(chunk, peer, my_row).wait_send()
        return carry

    def drain_col(chunk, carry):
        for peer in col_peers:
            col_copy(chunk, peer, my_col).wait_send()
        return carry

    lax.fori_loop(0, chunks, drain_row, 0)
    lax.fori_loop(chunks - SLOTS, chunks, drain_col, 0)


def form_beams(spectra, row_tab, col_tab, pols, row_size, col_size):
    _, units, local_cols, in_rows, width = spectra.shape
    nrow = row_tab.shape[0] // 2
    ncol = local_cols * col_size
    local_beams = nrow // col_size
    chunks = CHUNKS
    while units // pols % chunks and chunks > SLOTS + 1:
        chunks //= 2
    size = units // chunks
    vmem = pl.BlockSpec(memory_space=pltpu.VMEM)
    return pl.pallas_call(
        functools.partial(beam_kernel, row_size, col_size, chunks),
        in_specs=[pl.BlockSpec(memory_space=pl.ANY), vmem, vmem],
        out_specs=vmem,
        out_shape=jax.ShapeDtypeStruct((pols, local_beams * ncol, width), F32),
        scratch_shapes=[
            pltpu.VMEM((row_size, units, local_cols, in_rows, width), BF16),
            pltpu.VMEM((SLOTS, col_size, size, local_cols, 2 * local_beams, width), BF16),
            pltpu.VMEM((col_size, units, local_cols, 2 * local_beams, width), BF16),
            pltpu.SemaphoreType.DMA((chunks, row_size)),
            pltpu.SemaphoreType.DMA((chunks, row_size)),
            pltpu.SemaphoreType.DMA((chunks,)),
            pltpu.SemaphoreType.DMA((chunks, col_size)),
            pltpu.SemaphoreType.DMA((chunks, col_size)),
            pltpu.SemaphoreType.DMA((chunks,)),
        ],
        compiler_params=pltpu.CompilerParams(
            collective_id=0, has_side_effects=True, vmem_limit_bytes=VMEM_BYTES
        ),
        name="form_beams",
    )(spectra, row_tab, col_tab)


def body(voltages, fir):
    taps, nchan = fir.shape
    comps, local_rows, local_cols, pols, samples = voltages.shape
    row_size = lax.axis_size("row")
    col_size = lax.axis_size("col")
    nrow, ncol = local_rows * row_size, local_cols * col_size
    blocks = samples // nchan
    frames = blocks - taps + 1
    local_beams = nrow // col_size
    width = nchan // row_size
    volts = voltages.reshape(comps, local_rows, local_cols, pols, blocks, nchan)
    volts = volts.transpose(3, 2, 0, 4, 1, 5)
    spectra = channelize(volts, fir, jnp.asarray(channel_table(nchan, row_size)), row_size)
    spectra = spectra.reshape(row_size, pols * frames, local_cols, 2 * local_rows, width)
    power = form_beams(
        spectra,
        jnp.asarray(row_table(nrow, row_size, col_size)),
        jnp.asarray(col_table(ncol, col_size, local_beams)),
        pols, row_size, col_size,
    )
    scale = 1.0 / (frames * nrow * ncol)
    power = power.reshape(pols, local_beams, ncol, width) * scale
    return power.transpose(1, 2, 0, 3)


def solution(mesh):
    in_specs = (P(None, "row", "col", None, None), P())
    out_specs = P("col", None, None, "row")
    return jax.shard_map(body, mesh=mesh, in_specs=in_specs, out_specs=out_specs, check_vma=False)
```

```python
import functools
import math

import jax
import jax.numpy as jnp
import numpy as np
import ml_dtypes
from jax import lax
from jax.experimental import pallas as pl
from jax.experimental.pallas import tpu as pltpu
from jax.sharding import PartitionSpec as P

BF16 = jnp.bfloat16
F32 = jnp.float32
MESH = pl.DeviceIdType.MESH
VMEM_BYTES = 62 * 1024 * 1024
SLOTS = 3


def fourier_parts(length):
    index = np.arange(length)
    angle = (index[:, None] * index[None, :] % length).astype(np.float32) * np.float32(
        2.0 * math.pi / length
    )
    return np.cos(angle), np.sin(angle)


def channel_table(nchan):
    cosine, sine = fourier_parts(nchan)
    return np.concatenate([cosine, sine]).astype(ml_dtypes.bfloat16)


def spatial_parts(length):
    cosine, sine = fourier_parts(length)
    table = np.stack([np.stack([cosine, -sine]), np.stack([sine, cosine])])
    return table.astype(ml_dtypes.bfloat16)


def row_table(nrow, row_size, col_size):
    table = spatial_parts(nrow).reshape(2, 2, col_size, nrow // col_size, row_size, nrow // row_size)
    return table.transpose(2, 1, 3, 4, 0, 5).reshape(2 * nrow, 2 * nrow)


def col_table(ncol, col_size, local_beams):
    table = spatial_parts(ncol).astype(np.float32)
    eye = np.eye(local_beams, dtype=np.float32)
    full = np.einsum("cdvb,uw->duvbcw", table, eye)
    return full.reshape(2 * local_beams * ncol, ncol * 2 * local_beams).astype(ml_dtypes.bfloat16)


def beam_kernel(
    row_size, col_size, volts, fir, table, row_tab, col_tab, power,
    raw, spread, held, row_send, row_recv, col_send, col_recv,
    raw_sem, row_send_sem, row_recv_sem, row_own_sem, col_send_sem, col_recv_sem, col_own_sem,
):
    my_row = lax.axis_index("row")
    my_col = lax.axis_index("col")
    _, rows, local_cols, pols, _ = volts.shape
    taps, nchan = fir.shape
    blocks = spread.shape[0]
    frames = blocks - taps + 1
    lanes = spread.shape[3]
    tiles = nchan // lanes
    width = nchan // row_size
    out_rows = power.shape[1]
    chunks = pols * local_cols
    row_peers = [lax.rem(my_row + step, row_size) for step in range(1, row_size)]
    col_peers = [lax.rem(my_col + step, col_size) for step in range(1, col_size)]

    def raw_copy(chunk, comp):
        return pltpu.make_async_copy(
            volts.at[comp, :, lax.rem(chunk, local_cols)], raw.at[comp], raw_sem.at[comp]
        )

    def row_copy(chunk, peer, source):
        return pltpu.make_async_remote_copy(
            src_ref=row_send.at[lax.rem(chunk, SLOTS), peer],
            dst_ref=row_recv.at[source, chunk],
            send_sem=row_send_sem.at[chunk, peer],
            recv_sem=row_recv_sem.at[chunk, source],
            device_id={"row": peer},
            device_id_type=MESH,
        )

    def row_own(chunk):
        return pltpu.make_async_copy(
            row_send.at[lax.rem(chunk, SLOTS), my_row],
            row_recv.at[my_row, chunk],
            row_own_sem.at[chunk],
        )

    def col_copy(chunk, peer, source):
        return pltpu.make_async_remote_copy(
            src_ref=col_send.at[lax.rem(chunk, SLOTS), peer],
            dst_ref=col_recv.at[source, chunk],
            send_sem=col_send_sem.at[chunk, peer],
            recv_sem=col_recv_sem.at[chunk, source],
            device_id={"col": peer},
            device_id_type=MESH,
        )

    def col_own(chunk):
        return pltpu.make_async_copy(
            col_send.at[lax.rem(chunk, SLOTS), my_col],
            col_recv.at[my_col, chunk],
            col_own_sem.at[chunk],
        )

    def channelize(chunk):
        pol = chunk // local_cols
        for comp in range(2):
            raw_copy(chunk, comp).wait()

            def spread_step(block, carry):
                start = pl.multiple_of(block * nchan, nchan)
                for row in range(rows):
                    pair = raw[comp, row, :, pl.ds(start, nchan)].astype(F32)
                    for tile in range(tiles):
                        spread[block, tile, pl.ds(row, pols, stride=rows), :] = pair[
                            :, tile * lanes : (tile + 1) * lanes
                        ]
                return carry

            lax.fori_loop(0, blocks, spread_step, 0)

            @pl.when(chunk + 1 < chunks)
            def _():
                raw_copy(chunk + 1, comp).start()

            def filter_step(tile, carry):
                start = pl.multiple_of(tile * lanes, lanes)
                weights = [
                    jnp.broadcast_to(fir[pl.ds(tap, 1), pl.ds(start, lanes)], (rows, lanes))
                    for tap in range(taps)
                ]
                first = pl.multiple_of(pol * rows, rows)
                values = [spread[block, tile, pl.ds(first, rows), :] for block in range(blocks)]
                for frame in range(frames):
                    total = values[frame] * weights[0]
                    for tap in range(1, taps):
                        total = total + values[frame + tap] * weights[tap]
                    held[frame, :, pl.ds(pl.multiple_of(comp * nchan + start, lanes), lanes)] = (
                        total.astype(BF16)
                    )
                    if comp == 0:
                        held[frame, :, pl.ds(pl.multiple_of(2 * nchan + start, lanes), lanes)] = (
                            -total
                        ).astype(BF16)
                return carry

            lax.fori_loop(0, tiles, filter_step, 0)

        @pl.when(chunk >= SLOTS)
        def _():
            for peer in row_peers:
                row_copy(chunk - SLOTS, peer, my_row).wait_send()

        slot = lax.rem(chunk, SLOTS)
        for comp in range(2):
            lead = held[:, :, comp * nchan : (comp + 2) * nchan].reshape(frames * rows, 2 * nchan)
            for dest in range(row_size):
                part = jnp.dot(
                    lead, table[:, dest * width : (dest + 1) * width], preferred_element_type=F32
                ).astype(BF16)
                row_send[slot, dest, :, comp * rows : (comp + 1) * rows, :] = part.reshape(
                    frames, rows, width
                )

        for peer in row_peers:
            row_copy(chunk, peer, my_row).start()
        row_own(chunk).start()

    def form_rows(chunk):
        for peer in row_peers:
            row_copy(chunk, peer, peer).wait_recv()
        row_own(chunk).wait()

        @pl.when(chunk >= SLOTS)
        def _():
            for peer in col_peers:
                col_copy(chunk - SLOTS, peer, my_col).wait_send()
            col_own(chunk - SLOTS).wait()

        slot = lax.rem(chunk, SLOTS)

        def frame_step(step, carry):
            for part in range(4):
                frame = step * 4 + part
                block = row_recv[:, chunk, frame].reshape(-1, width)
                beam = jnp.dot(row_tab[...], block, preferred_element_type=F32).astype(BF16)
                col_send[slot, :, frame] = beam.reshape(col_size, -1, width)
            return carry

        lax.fori_loop(0, frames // 4, frame_step, 0)
        for peer in col_peers:
            col_copy(chunk, peer, my_col).start()
        col_own(chunk).start()

    def combine(pol):
        def receive(chunk, carry):
            for peer in col_peers:
                col_copy(chunk, peer, peer).wait_recv()
            return carry

        lax.fori_loop(pol * local_cols, (pol + 1) * local_cols, receive, 0)

        def frame_step(frame, carry):
            block = col_recv[:, pol * local_cols : (pol + 1) * local_cols, frame].reshape(-1, width)
            real = jnp.dot(col_tab[:out_rows], block, preferred_element_type=F32)
            imag = jnp.dot(col_tab[out_rows:], block, preferred_element_type=F32)
            power[pol] += real * real + imag * imag
            return carry

        lax.fori_loop(0, frames, frame_step, 0)

    for comp in range(2):
        raw_copy(0, comp).start()
    barrier = pltpu.get_barrier_semaphore()
    for peer in row_peers:
        pl.semaphore_signal(barrier, inc=1, device_id={"row": peer}, device_id_type=MESH)
    for peer in col_peers:
        pl.semaphore_signal(barrier, inc=1, device_id={"col": peer}, device_id_type=MESH)
    pl.semaphore_wait(barrier, row_size + col_size - 2)
    power[...] = jnp.zeros_like(power)

    def chunk_step(chunk, carry):
        @pl.when(chunk < chunks)
        def _():
            channelize(chunk)

        @pl.when(chunk >= 1)
        def _():
            form_rows(chunk - 1)

        for pol in range(pols - 1):
            @pl.when(chunk == (pol + 1) * local_cols + SLOTS)
            def _():
                combine(pol)

        return carry

    lax.fori_loop(0, chunks + 1, chunk_step, 0)

    def drain(chunk, carry):
        for peer in row_peers:
            row_copy(chunk, peer, my_row).wait_send()
        for peer in col_peers:
            col_copy(chunk, peer, my_col).wait_send()
        col_own(chunk).wait()
        return carry

    lax.fori_loop(chunks - SLOTS, chunks, drain, 0)
    combine(pols - 1)


def form_beams(voltages, fir, table, row_tab, col_tab, row_size, col_size):
    _, rows, local_cols, pols, samples = voltages.shape
    taps, nchan = fir.shape
    blocks = samples // nchan
    frames = blocks - taps + 1
    width = nchan // row_size
    lanes = 128
    ncol = local_cols * col_size
    local_beams = rows * row_size // col_size
    chunks = pols * local_cols
    vmem = pl.BlockSpec(memory_space=pltpu.VMEM)
    return pl.pallas_call(
        functools.partial(beam_kernel, row_size, col_size),
        in_specs=[pl.BlockSpec(memory_space=pl.ANY), vmem, vmem, vmem, vmem],
        out_specs=vmem,
        out_shape=jax.ShapeDtypeStruct((pols, local_beams * ncol, width), F32),
        scratch_shapes=[
            pltpu.VMEM((2, rows, pols, samples), BF16),
            pltpu.VMEM((blocks, nchan // lanes, pols * rows, lanes), F32),
            pltpu.VMEM((frames, rows, 3 * nchan), BF16),
            pltpu.VMEM((SLOTS, row_size, frames, 2 * rows, width), BF16),
            pltpu.VMEM((row_size, chunks, frames, 2 * rows, width), BF16),
            pltpu.VMEM((SLOTS, col_size, frames, 2 * local_beams, width), BF16),
            pltpu.VMEM((col_size, chunks, frames, 2 * local_beams, width), BF16),
            pltpu.SemaphoreType.DMA((2,)),
            pltpu.SemaphoreType.DMA((chunks, row_size)),
            pltpu.SemaphoreType.DMA((chunks, row_size)),
            pltpu.SemaphoreType.DMA((chunks,)),
            pltpu.SemaphoreType.DMA((chunks, col_size)),
            pltpu.SemaphoreType.DMA((chunks, col_size)),
            pltpu.SemaphoreType.DMA((chunks,)),
        ],
        compiler_params=pltpu.CompilerParams(
            collective_id=0, has_side_effects=True, vmem_limit_bytes=VMEM_BYTES
        ),
        name="form_beams",
    )(voltages, fir, table, row_tab, col_tab)


def body(voltages, fir):
    taps, nchan = fir.shape
    _, local_rows, local_cols, pols, samples = voltages.shape
    row_size = lax.axis_size("row")
    col_size = lax.axis_size("col")
    nrow, ncol = local_rows * row_size, local_cols * col_size
    frames = samples // nchan - taps + 1
    local_beams = nrow // col_size
    power = form_beams(
        voltages, fir,
        jnp.asarray(channel_table(nchan)),
        jnp.asarray(row_table(nrow, row_size, col_size)),
        jnp.asarray(col_table(ncol, col_size, local_beams)),
        row_size, col_size,
    )
    scale = 1.0 / (frames * nrow * ncol)
    power = power.reshape(pols, local_beams, ncol, nchan // row_size) * scale
    return power.transpose(1, 2, 0, 3)


def solution(mesh):
    in_specs = (P(None, "row", "col", None, None), P())
    out_specs = P("col", None, None, "row")
    return jax.shard_map(body, mesh=mesh, in_specs=in_specs, out_specs=out_specs, check_vma=False)
```
